32 devices in a mesh: groups: 2 (over y), blk: 4 (over z), store: 4 (over x, core).
Axes of the slice: x: 2, y: 2, z: 4, core: 2. Of those that a mesh axis runs over, the one named last changes fastest.
Arguments:
- embeddings: float32 [32768, 1024], P(('groups', 'blk', 'store')), parts along dimension 0, may hold values from -6 to 6
- slots: int32 [32768], P(('groups', 'blk', 'store')), parts along dimension 0, may hold values from 0 to 1023, as said below
- clusters: int32 [8, 4096], P(('groups', 'store'), 'blk'), parts along dimension 0, may hold values from 0 to 31, never falling along the last dimension, each value on 1 to 2048 neighbouring positions
- priority: int32 [8, 4096], P(('groups', 'store'), 'blk'), parts along dimension 0, may hold values from 0 to 4095, each once within a row
Outputs:
- nearest_earlier: float32 [32768], P(('groups', 'blk', 'store')), parts along dimension 0
The draws below stay inside these ranges and needn't reach their ends.
There are 2 independent parts, one for each index of `groups`. The reference program is written for one: setup_inputs(seed, part) draws one part's arguments, and reference() takes and returns one part's arrays. A program takes and returns all parts, laid end to end along the dimension named above; each array names one. Nothing has to cross between parts.
Inputs may be any that keep to these rules, and one draw needn't show every extreme that they name: For each panel of each owner, the slots of the 1024 storage rows bound for it are 0 to 1023, each once. `clusters`: in each owner's row the cluster numbers never fall, every number is used, and a cluster holds 1 to 2048 items, one exactly 2048. `priority`: each owner's row is a permutation.
All inputs are finite; a program needn't handle non-finite values.
Results may differ from the reference program's by a relative error of at most 0.0011.
Values may be sent and summed in bfloat16 or wider, within the bound.
A program may use at most 64 MiB of HBM per device.

```python
import math
import jax
import jax.numpy as jnp
import numpy as np
from jax import lax

D = 1024
ROWS = 1024
CL_OWN = 32
SPAN = 2
OWNERS = 4
PANELS = 4
SEND = 256
LOOP_ROWS = 4096
ITEMS = 16384
MOST = 2048


def draw_slots(key, part):
    key = jax.random.fold_in(key, 11)
    subkeys = jax.random.split(key, PANELS * OWNERS)
    shuffled = jax.vmap(lambda single: jax.random.permutation(single, ROWS))(subkeys)
    shuffled = shuffled.reshape(PANELS, OWNERS, OWNERS, SEND)
    return jnp.transpose(shuffled, (0, 2, 1, 3)).reshape(-1).astype(jnp.int32)


def block_scale(rng, dims, cuts, smallest, largest):
    def one(dim, blocks):
        draws = jax.random.uniform(jax.random.fold_in(jax.random.fold_in(rng, 6), dim), (blocks,), jnp.float32, smallest / len(cuts), largest / len(cuts))
        return jnp.repeat(jnp.exp(draws), dims[dim] // blocks).reshape((-1,) + (1,) * (len(dims) - dim - 1))

    level = one(*cuts[0])
    for cut in cuts[1:]:
        level = level * one(*cut)
    return level


def split_up(count, total, bound, slope):
    weights = [(1 << 20) // math.isqrt(rank ** slope) + 1 for rank in range(2, count + 1)]
    spare, holding = total - bound - (count - 1), [1] * (count - 1)
    while spare > 0:
        movable = [i for i in range(count - 1) if holding[i] < bound]
        pool, left = sum([weights[i] for i in movable]), spare
        for i in movable:
            extra = min(bound - holding[i], max(1, left * weights[i] // pool), spare)
            holding[i] = holding[i] + extra
            spare = spare - extra
    return np.array([bound] + holding)


def ragged(key, number_of, total, reach, slope):
    if number_of == 2:
        one = jax.random.randint(key, (), max(1, total - reach), min(reach, total - 1) + 1)
        return jnp.stack([one, total - one])
    tallies = jnp.asarray(split_up(number_of, total, reach, slope), jnp.int32)
    pairs = (number_of - 1) // 2
    donor, receiver = tallies[1:1 + 2 * pairs:2], tallies[2:2 + 2 * pairs:2]
    slack = jnp.minimum(donor - 1, reach - receiver)
    shifted = jax.random.randint(jax.random.fold_in(key, 1), (pairs,), 0, 1 << 20) % (slack + 1)
    tallies = tallies.at[1:1 + 2 * pairs:2].set(donor - shifted).at[2:2 + 2 * pairs:2].set(receiver + shifted)
    return tallies[jax.random.permutation(jax.random.fold_in(key, 2), number_of)]


def bell_draw(stream_key, shape, scale, reach, cuts=(), held_as=jnp.bfloat16):
    result = scale * jax.random.normal(stream_key, shape, jnp.float32)
    if cuts:
        result = result * block_scale(stream_key, shape, cuts, -0.22, 0.18)
    return jnp.clip(result, -reach, reach).astype(held_as)


def setup_inputs(seed: int = 0, part: int = 0) -> dict:
    arg_keys = jax.random.split(jax.random.key(seed), 5)
    own_keys = jax.random.split(jax.random.fold_in(arg_keys[4], part), 5)
    return {
        "embeddings": bell_draw(own_keys[0], (ITEMS, D), 1.0, 6.0, ((0, 16),), jnp.float32),
        "slots": draw_slots(jax.random.fold_in(jax.random.fold_in(arg_keys[4], part), 71), part),
        "clusters": jax.vmap(lambda own: jnp.searchsorted(jnp.cumsum(ragged(own, CL_OWN, LOOP_ROWS, MOST, 2)), jnp.arange(LOOP_ROWS), side="right"))(jax.random.split(own_keys[2], OWNERS)).reshape((OWNERS, LOOP_ROWS)).astype(jnp.int32),
        "priority": jax.vmap(lambda own: jax.random.permutation(own, LOOP_ROWS))(jax.random.split(own_keys[3], OWNERS)).reshape((OWNERS, LOOP_ROWS)).astype(jnp.int32),
    }


EPS = 1e-06

def reference(embeddings, slots, clusters, priority):
    unit_rows = (embeddings * lax.rsqrt(lax.optimization_barrier(jnp.sum(embeddings * embeddings, axis=1, keepdims=True)) + EPS)).astype(jnp.bfloat16)
    item_index = jnp.arange(ITEMS, dtype=jnp.int32)
    owner_of = item_index % ROWS // SEND
    panel_of = item_index // ROWS // OWNERS
    position = panel_of * ROWS + slots
    placed = jnp.zeros((OWNERS, LOOP_ROWS, D), jnp.bfloat16).at[owner_of, position].set(unit_rows)
    margin = SPAN * ROWS
    padded = jnp.pad(placed, ((0, 0), (margin, margin), (0, 0)))
    labels = jnp.pad(clusters + 1, ((0, 0), (margin, margin)))
    ranking = jnp.pad(priority, ((0, 0), (margin, margin)))
    span_rows = (2 * SPAN + 1) * ROWS

    def one_panel(flat):
        owner_at = (flat // PANELS).astype(jnp.int32)
        row_start = (flat % PANELS * ROWS).astype(jnp.int32)
        anchor = jnp.int32(0)
        window = lax.dynamic_slice(padded, (owner_at, row_start, anchor), (1, span_rows, D))[0]
        window_labels = lax.dynamic_slice(labels, (owner_at, row_start), (1, span_rows))[0]
        window_rank = lax.dynamic_slice(ranking, (owner_at, row_start), (1, span_rows))[0]
        own_rows = window[margin:margin + ROWS]
        own_labels = window_labels[margin:margin + ROWS]
        own_rank = window_rank[margin:margin + ROWS]
        scores = jnp.dot(own_rows, window.T, preferred_element_type=jnp.float32)
        same_pair = (own_labels[:, None] == window_labels[None, :]) & (window_rank[None, :] < own_rank[:, None])
        return lax.optimization_barrier(jnp.max(jnp.where(same_pair, scores, -1.0), axis=1))
    best_owner = lax.map(one_panel, jnp.arange(OWNERS * PANELS, dtype=jnp.int32)).reshape(OWNERS, LOOP_ROWS)
    return best_owner[owner_of, position]
```

```python
import functools

import jax
import jax.numpy as jnp
from jax import lax
from jax.experimental import pallas as pl
from jax.experimental.pallas import tpu as pltpu
from jax.sharding import PartitionSpec as P

EPS = 1e-06
MESH = pl.DeviceIdType.MESH


def kernel(
    panels,
    stores,
    emb_ref,
    slots_ref,
    cl_ref,
    pr_ref,
    out_ref,
    emb,
    mine,
    left,
    right,
    bound,
    slots_in,
    tag_mine,
    tag_left,
    tag_right,
    clcol_mine,
    prcol_mine,
    clcol_left,
    prcol_left,
    row_mine,
    row_left,
    col_mine,
    col_right,
    back_mine,
    back_left,
    back_right,
    home,
    load_sem,
    st_send,
    st_recv,
    sl_send,
    sl_recv,
    tg_send,
    tg_recv,
    zl_send,
    zl_recv,
    zr_send,
    zr_recv,
    bk_send,
    bk_recv,
):
    rows, width = emb.shape[0] * emb.shape[1], emb.shape[2]
    send = rows // stores
    half = stores // 2
    p = lax.axis_index("blk")
    s = lax.axis_index("store")

    def out_peer(d):
        return lax.rem(s // 2 + d // 2, half) * 2 + lax.rem(lax.rem(s, 2) + d % 2, 2)

    def in_peer(d):
        return lax.rem(s // 2 + half - d // 2, half) * 2 + lax.rem(lax.rem(s, 2) + d % 2, 2)

    has_prev = p >= 1
    has_next = p <= panels - 2
    use_right = has_next
    use_left = jnp.logical_and(has_prev, has_next)
    give_right = p <= panels - 3
    give_left = has_prev

    barrier = pltpu.get_barrier_semaphore()
    for d in range(1, stores):
        pl.semaphore_signal(barrier, inc=1, device_id={"store": out_peer(d)}, device_id_type=MESH)

    @pl.when(has_prev)
    def _():
        for d in range(stores):
            pl.semaphore_signal(
                barrier, inc=1, device_id={"blk": p - 1, "store": out_peer(d)}, device_id_type=MESH
            )

    @pl.when(has_next)
    def _():
        for d in range(stores):
            pl.semaphore_signal(
                barrier, inc=1, device_id={"blk": p + 1, "store": out_peer(d)}, device_id_type=MESH
            )

    order = [2, 0, 1] + list(range(3, stores)) if stores > 2 else [0, 1]

    def load(d):
        return pltpu.make_async_copy(
            emb_ref.at[pl.ds(pl.multiple_of(out_peer(d) * send, send), send)],
            emb.at[d],
            load_sem.at[d],
        )

    for d in order:
        load(d).start()

    low = jnp.full((1, send), -1.0, jnp.float32)
    for k in range(3):
        for o in range(stores):
            home[k, o] = low
    for ref in (row_mine, row_left):
        ref[...] = jnp.full(ref.shape, -1.0, jnp.float32)
    for ref in (col_mine, col_right):
        ref[...] = jnp.full(ref.shape, -1.0, jnp.float32)

    def store_copy(d):
        return pltpu.make_async_remote_copy(
            src_ref=bound.at[d],
            dst_ref=mine.at[d],
            send_sem=st_send.at[d],
            recv_sem=st_recv.at[d],
            device_id={"store": out_peer(d)},
            device_id_type=MESH,
        )

    def slot_copy(d):
        return pltpu.make_async_remote_copy(
            src_ref=slots_ref.at[:, pl.ds(pl.multiple_of(out_peer(d) * send, send), send)],
            dst_ref=slots_in.at[d],
            send_sem=sl_send.at[d],
            recv_sem=sl_recv.at[d],
            device_id={"store": out_peer(d)},
            device_id_type=MESH,
        )

    def to_left(d):
        return pltpu.make_async_remote_copy(
            src_ref=mine.at[d],
            dst_ref=right.at[d],
            send_sem=zl_send.at[d],
            recv_sem=zl_recv.at[d],
            device_id={"blk": p - 1},
            device_id_type=MESH,
        )

    def to_right(d):
        return pltpu.make_async_remote_copy(
            src_ref=mine.at[d],
            dst_ref=left.at[d],
            send_sem=zr_send.at[d],
            recv_sem=zr_recv.at[d],
            device_id={"blk": p + 1},
            device_id_type=MESH,
        )

    def tag_copy(to_next):
        return pltpu.make_async_remote_copy(
            src_ref=tag_mine,
            dst_ref=tag_left if to_next else tag_right,
            send_sem=tg_send.at[1 if to_next else 0],
            recv_sem=tg_recv.at[1 if to_next else 0],
            device_id={"blk": p + 1 if to_next else p - 1},
            device_id_type=MESH,
        )

    def forward(d):
        @pl.when(give_right)
        def _():
            to_right(d).start()

        @pl.when(give_left)
        def _():
            to_left(d).start()

    def normalize(d):
        load(d).wait()
        x = emb[d]
        unit = (x * lax.rsqrt(jnp.sum(x * x, axis=1, keepdims=True) + EPS)).astype(jnp.bfloat16)
        if d == 0:
            mine[0] = unit
        else:
            bound[d] = unit

    for number, d in enumerate(order):
        normalize(d)
        if number == 0:
            here = jnp.int32(stores - 1)
            here = here + jnp.where(has_prev, stores, 0) + jnp.where(has_next, stores, 0)
            pl.semaphore_wait(barrier, here)
            for e in range(1, stores):
                slot_copy(e).start()
        if d == 0:
            forward(0)
        else:
            store_copy(d).start()

    clusters = cl_ref[...].astype(jnp.float32)
    rank = pr_ref[...]
    upper = (rank // 128).astype(jnp.float32)
    lower = (rank - rank // 128 * 128).astype(jnp.float32)
    line = lax.broadcasted_iota(jnp.int32, (16, rows), 0)
    table = jnp.where(
        line == 0, clusters, jnp.where(line == 1, upper, jnp.where(line == 2, lower, 0.0))
    ).astype(jnp.bfloat16)

    def columns(tag_ref, clcol, prcol, d):
        clcol[d] = jnp.transpose(jnp.broadcast_to(tag_ref[d, 0:1, :], (128, send)))
        prcol[d] = jnp.transpose(jnp.broadcast_to(tag_ref[d, 1:2, :], (128, send)))

    slots_in[0] = slots_ref[:, pl.ds(pl.multiple_of(s * send, send), send)]
    for d in range(stores):
        if d > 0:
            slot_copy(d).wait()
        hot = jnp.where(
            lax.broadcasted_iota(jnp.int32, (rows, send), 0) == slots_in[d], 1.0, 0.0
        ).astype(jnp.bfloat16)
        found = jnp.dot(table, hot, preferred_element_type=jnp.float32)
        tag_mine[d] = jnp.concatenate(
            [found[0:1], found[1:2] * 128.0 + found[2:3], found[2:8]], axis=0
        )
        columns(tag_mine, clcol_mine, prcol_mine, d)

    @pl.when(give_right)
    def _():
        tag_copy(True).start()

    @pl.when(give_left)
    def _():
        tag_copy(False).start()

    def pair(a_ref, i, clcol, prcol, row_acc, b_ref, j, tag_ref, col_acc):
        scores = lax.dot_general(
            a_ref[i], b_ref[j], (((1,), (1,)), ((), ())), preferred_element_type=jnp.float32
        )
        cl_r, pr_r = clcol[i], prcol[i]
        best = row_acc[i]
        for k in range(send // 128):
            part = slice(k * 128, (k + 1) * 128)
            cl_q = tag_ref[j, 0:1, part]
            pr_q = tag_ref[j, 1:2, part]
            same = jnp.where(cl_r == cl_q, scores[:, part], -1.0)
            best = jnp.maximum(best, jnp.where(pr_q < pr_r, same, -1.0))
            other = jnp.where(pr_q > pr_r, same, -1.0)
            top = jnp.max(other.reshape(send // 8, 8, 128), axis=0)
            col_acc[j, :, part] = jnp.maximum(col_acc[j, :, part], top)
        row_acc[i] = best

    def loop(count, step):
        def each(i, carry):
            step(i)
            return carry

        lax.fori_loop(0, count, each, 0)

    for d in range(stores):
        if d > 0:
            store_copy(d).wait_recv()
            forward(d)
        loop(
            d + 1,
            lambda i, d=d: pair(
                mine, i, clcol_mine, prcol_mine, row_mine, mine, d, tag_mine, col_mine
            ),
        )

    def finish(acc_row, acc_col, d):
        parts = []
        if acc_row is not None:
            parts.append(jnp.max(jnp.transpose(acc_row[d]), axis=0, keepdims=True))
        if acc_col is not None:
            parts.append(jnp.max(acc_col[d], axis=0, keepdims=True))
        return functools.reduce(jnp.maximum, parts)

    def back_copy(kind, src, d):
        where = {"store": in_peer(d)}
        if kind:
            where["blk"] = p + 1 if kind == 1 else p - 1
        return pltpu.make_async_remote_copy(
            src_ref=src.at[d],
            dst_ref=home.at[kind, s],
            send_sem=bk_send.at[kind, d],
            recv_sem=bk_recv.at[kind, s],
            device_id=where,
            device_id_type=MESH,
        )

    @pl.when(use_left)
    def _():
        tag_copy(True).wait_recv()
        for d in range(stores):
            columns(tag_left, clcol_left, prcol_left, d)

    @pl.when(use_right)
    def _():
        tag_copy(False).wait_recv()

    for d in range(stores):

        @pl.when(use_right)
        def _(d=d):
            to_left(d).wait_recv()
            loop(
                stores,
                lambda i: pair(
                    mine, i, clcol_mine, prcol_mine, row_mine, right, d, tag_right, col_right
                ),
            )

        if d == stores - 1:
            for e in range(stores):
                back_mine[e] = finish(row_mine, col_mine, e)
            for e in range(1, stores):
                back_copy(0, back_mine, e).start()
            home[0, s] = back_mine[0]

        @pl.when(use_left)
        def _(d=d):
            to_right(d).wait_recv()
            loop(
                d + 1,
                lambda i: pair(
                    left, i, clcol_left, prcol_left, row_left, right, d, tag_right, col_right
                ),
            )
            if d > 0:
                loop(
                    d,
                    lambda j: pair(
                        left, d, clcol_left, prcol_left, row_left, right, j, tag_right, col_right
                    ),
                )

    @pl.when(use_right)
    def _():
        for e in range(stores):
            back_right[e] = finish(None, col_right, e)
            back_copy(1, back_right, e).start()

    @pl.when(use_left)
    def _():
        for e in range(stores):
            back_left[e] = finish(row_left, None, e)
            back_copy(2, back_left, e).start()

    for d in range(1, stores):
        store_copy(d).wait_send()

    @pl.when(give_right)
    def _():
        tag_copy(True).wait_send()
        for d in range(stores):
            to_right(d).wait_send()

    @pl.when(give_left)
    def _():
        tag_copy(False).wait_send()
        for d in range(stores):
            to_left(d).wait_send()

    def arrived(kind, o):
        return pltpu.make_async_remote_copy(
            src_ref=back_mine.at[0],
            dst_ref=home.at[kind, o],
            send_sem=bk_send.at[kind, 0],
            recv_sem=bk_recv.at[kind, o],
            device_id={"store": out_peer(1)},
            device_id_type=MESH,
        )

    for d in range(1, stores):
        back_copy(0, back_mine, d).wait_send()
        arrived(0, out_peer(d)).wait_recv()

    @pl.when(use_right)
    def _():
        for d in range(stores):
            back_copy(1, back_right, d).wait_send()

    @pl.when(use_left)
    def _():
        for d in range(stores):
            back_copy(2, back_left, d).wait_send()

    @pl.when(has_prev)
    def _():
        for o in range(stores):
            arrived(1, o).wait_recv()

    @pl.when(give_right)
    def _():
        for o in range(stores):
            arrived(2, o).wait_recv()

    for o in range(stores):
        out_ref[:, o * send : (o + 1) * send] = jnp.maximum(
            home[0, o], jnp.maximum(home[1, o], home[2, o])
        )


def solution(mesh):
    panels, stores = mesh.shape["blk"], mesh.shape["store"]

    def body(embeddings, slots, clusters, priority):
        rows, width = embeddings.shape
        send = rows // stores
        f32, bf16, i32 = jnp.float32, jnp.bfloat16, jnp.int32
        vm = pltpu.VMEM
        dma = pltpu.SemaphoreType.DMA
        best = pl.pallas_call(
            functools.partial(kernel, panels, stores),
            out_shape=jax.ShapeDtypeStruct((1, rows), f32),
            in_specs=[
                pl.BlockSpec(memory_space=pl.ANY),
                pl.BlockSpec(memory_space=vm),
                pl.BlockSpec(memory_space=vm),
                pl.BlockSpec(memory_space=vm),
            ],
            out_specs=pl.BlockSpec(memory_space=vm),
            scratch_shapes=[
                vm((stores, send, width), f32),
                vm((stores, send, width), bf16),
                vm((stores, send, width), bf16),
                vm((stores, send, width), bf16),
                vm((stores, send, width), bf16),
                vm((stores, 1, send), i32),
                vm((stores, 8, send), f32),
                vm((stores, 8, send), f32),
                vm((stores, 8, send), f32),
                vm((stores, send, 128), f32),
                vm((stores, send, 128), f32),
                vm((stores, send, 128), f32),
                vm((stores, send, 128), f32),
                vm((stores, send, 128), f32),
                vm((stores, send, 128), f32),
                vm((stores, 8, send), f32),
                vm((stores, 8, send), f32),
                vm((stores, 1, send), f32),
                vm((stores, 1, send), f32),
                vm((stores, 1, send), f32),
                vm((3, stores, 1, send), f32),
                dma((stores,)),
                dma((stores,)),
                dma((stores,)),
                dma((stores,)),
                dma((stores,)),
                dma((2,)),
                dma((2,)),
                dma((stores,)),
                dma((stores,)),
                dma((stores,)),
                dma((stores,)),
                dma((3, stores)),
                dma((3, stores)),
            ],
            compiler_params=pltpu.CompilerParams(
                collective_id=0, has_side_effects=True, vmem_limit_bytes=48 * 1024 * 1024
            ),
            name="dedup",
        )(embeddings, slots.reshape(1, rows), clusters, priority)
        return best.reshape(rows)

    return jax.shard_map(
        body,
        mesh=mesh,
        in_specs=(
            P(("groups", "blk", "store"), None),
            P(("groups", "blk", "store")),
            P(("groups", "store"), "blk"),
            P(("groups", "store"), "blk"),
        ),
        out_specs=P(("groups", "blk", "store")),
        check_vma=False,
    )
```

```python
import functools

import jax
import jax.numpy as jnp
from jax import lax
from jax.experimental import pallas as pl
from jax.experimental.pallas import tpu as pltpu
from jax.sharding import PartitionSpec as P

EPS = 1e-06
MESH = pl.DeviceIdType.MESH


def kernel(
    panels,
    stores,
    emb_ref,
    slots_hbm,
    cl_hbm,
    pr_hbm,
    out_ref,
    slots_ref,
    cl_ref,
    pr_ref,
    emb,
    mine,
    left,
    right,
    bound,
    slots_in,
    tag_mine,
    tag_left,
    tag_right,
    clcol_mine,
    prcol_mine,
    clcol_left,
    prcol_left,
    row_mine,
    row_left,
    col_mine,
    col_right,
    back_mine,
    back_left,
    back_right,
    home,
    load_sem,
    small_sem,
    st_send,
    st_recv,
    sl_send,
    sl_recv,
    tg_send,
    tg_recv,
    zl_send,
    zl_recv,
    zr_send,
    zr_recv,
    bk_send,
    bk_recv,
):
    rows, width = emb.shape[0] * emb.shape[1], emb.shape[2]
    send = rows // stores
    half = stores // 2
    p = lax.axis_index("blk")
    s = lax.axis_index("store")

    def out_peer(d):
        return lax.rem(s // 2 + d // 2, half) * 2 + lax.rem(lax.rem(s, 2) + d % 2, 2)

    def in_peer(d):
        return lax.rem(s // 2 + half - d // 2, half) * 2 + lax.rem(lax.rem(s, 2) + d % 2, 2)

    has_prev = p >= 1
    has_next = p <= panels - 2
    use_right = has_next
    use_left = jnp.logical_and(has_prev, has_next)
    give_right = p <= panels - 3
    give_left = has_prev

    barrier = pltpu.get_barrier_semaphore()
    for d in range(1, stores):
        pl.semaphore_signal(barrier, inc=1, device_id={"store": out_peer(d)}, device_id_type=MESH)

    @pl.when(has_prev)
    def _():
        for d in range(stores):
            pl.semaphore_signal(
                barrier, inc=1, device_id={"blk": p - 1, "store": out_peer(d)}, device_id_type=MESH
            )

    @pl.when(has_next)
    def _():
        for d in range(stores):
            pl.semaphore_signal(
                barrier, inc=1, device_id={"blk": p + 1, "store": out_peer(d)}, device_id_type=MESH
            )

    order = [0, 2, 1] + list(range(3, stores)) if stores > 2 else [0, 1]

    def load(d):
        return pltpu.make_async_copy(
            emb_ref.at[pl.ds(pl.multiple_of(out_peer(d) * send, send), send)],
            emb.at[d],
            load_sem.at[d],
        )

    small = [
        pltpu.make_async_copy(a, b, small_sem.at[k])
        for k, (a, b) in enumerate(
            [(slots_hbm, slots_ref), (cl_hbm, cl_ref), (pr_hbm, pr_ref)]
        )
    ]
    for d in order:
        load(d).start()
    for copy in small:
        copy.start()

    low = jnp.full((1, send), -1.0, jnp.float32)
    for k in range(3):
        for o in range(stores):
            home[k, o] = low
    for ref in (row_mine, row_left):
        ref[...] = jnp.full(ref.shape, -1.0, jnp.float32)
    for ref in (col_mine, col_right):
        ref[...] = jnp.full(ref.shape, -1.0, jnp.float32)

    def store_copy(d):
        return pltpu.make_async_remote_copy(
            src_ref=bound.at[d],
            dst_ref=mine.at[d],
            send_sem=st_send.at[d],
            recv_sem=st_recv.at[d],
            device_id={"store": out_peer(d)},
            device_id_type=MESH,
        )

    def slot_copy(d):
        return pltpu.make_async_remote_copy(
            src_ref=slots_ref.at[:, pl.ds(pl.multiple_of(out_peer(d) * send, send), send)],
            dst_ref=slots_in.at[d],
            send_sem=sl_send.at[d],
            recv_sem=sl_recv.at[d],
            device_id={"store": out_peer(d)},
            device_id_type=MESH,
        )

    def to_left(d):
        return pltpu.make_async_remote_copy(
            src_ref=mine.at[d],
            dst_ref=right.at[d],
            send_sem=zl_send.at[d],
            recv_sem=zl_recv.at[d],
            device_id={"blk": p - 1},
            device_id_type=MESH,
        )

    def to_right(d):
        return pltpu.make_async_remote_copy(
            src_ref=mine.at[d],
            dst_ref=left.at[d],
            send_sem=zr_send.at[d],
            recv_sem=zr_recv.at[d],
            device_id={"blk": p + 1},
            device_id_type=MESH,
        )

    def tag_copy(to_next):
        return pltpu.make_async_remote_copy(
            src_ref=tag_mine,
            dst_ref=tag_left if to_next else tag_right,
            send_sem=tg_send.at[1 if to_next else 0],
            recv_sem=tg_recv.at[1 if to_next else 0],
            device_id={"blk": p + 1 if to_next else p - 1},
            device_id_type=MESH,
        )

    def forward(d):
        @pl.when(give_right)
        def _():
            to_right(d).start()

        @pl.when(give_left)
        def _():
            to_left(d).start()

    def normalize(d):
        load(d).wait()
        x = emb[d]
        unit = (x * lax.rsqrt(jnp.sum(x * x, axis=1, keepdims=True) + EPS)).astype(jnp.bfloat16)
        if d == 0:
            mine[0] = unit
        else:
            bound[d] = unit

    for number, d in enumerate(order):
        normalize(d)
        if number == 0:
            here = jnp.int32(stores - 1)
            here = here + jnp.where(has_prev, stores, 0) + jnp.where(has_next, stores, 0)
            pl.semaphore_wait(barrier, here)
            small[0].wait()
            for e in range(1, stores):
                slot_copy(e).start()
        if d == 0:
            forward(0)
        else:
            store_copy(d).start()

    small[1].wait()
    small[2].wait()
    clusters = cl_ref[...].astype(jnp.float32)
    rank = pr_ref[...]
    upper = (rank // 128).astype(jnp.float32)
    lower = (rank - rank // 128 * 128).astype(jnp.float32)
    line = lax.broadcasted_iota(jnp.int32, (16, rows), 0)
    table = jnp.where(
        line == 0, clusters, jnp.where(line == 1, upper, jnp.where(line == 2, lower, 0.0))
    ).astype(jnp.bfloat16)

    def columns(tag_ref, clcol, prcol, d):
        clcol[d] = jnp.transpose(jnp.broadcast_to(tag_ref[d, 0:1, :], (128, send)))
        prcol[d] = jnp.transpose(jnp.broadcast_to(tag_ref[d, 1:2, :], (128, send)))

    slots_in[0] = slots_ref[:, pl.ds(pl.multiple_of(s * send, send), send)]
    for d in range(stores):
        if d > 0:
            slot_copy(d).wait()
        hot = jnp.where(
            lax.broadcasted_iota(jnp.int32, (rows, send), 0) == slots_in[d], 1.0, 0.0
        ).astype(jnp.bfloat16)
        found = jnp.dot(table, hot, preferred_element_type=jnp.float32)
        tag_mine[d] = jnp.concatenate(
            [found[0:1], found[1:2] * 128.0 + found[2:3], found[2:8]], axis=0
        )
        columns(tag_mine, clcol_mine, prcol_mine, d)

    @pl.when(give_right)
    def _():
        tag_copy(True).start()

    @pl.when(give_left)
    def _():
        tag_copy(False).start()

    def pairs(a_ref, i, n, clcol, prcol, row_acc, b_ref, j, m, tag_ref, col_acc):
        a = a_ref[pl.ds(i, n)].reshape(n * send, width)
        b = b_ref[pl.ds(j, m)].reshape(m * send, width)
        scores = lax.dot_general(
            a, b, (((1,), (1,)), ((), ())), preferred_element_type=jnp.float32
        )
        for x in range(n):
            cl_r, pr_r = clcol[i + x], prcol[i + x]
            best = row_acc[i + x]
            for y in range(m):
                for k in range(send // 128):
                    part = slice(k * 128, (k + 1) * 128)
                    cl_q = tag_ref[j + y, 0:1, part]
                    pr_q = tag_ref[j + y, 1:2, part]
                    piece = scores[
                        x * send : (x + 1) * send, y * send + k * 128 : y * send + (k + 1) * 128
                    ]
                    same = jnp.where(cl_r == cl_q, piece, -1.0)
                    best = jnp.maximum(best, jnp.where(pr_q < pr_r, same, -1.0))
                    other = jnp.where(pr_q > pr_r, same, -1.0)
                    top = jnp.max(other.reshape(send // 8, 8, 128), axis=0)
                    col_acc[j + y, :, part] = jnp.maximum(col_acc[j + y, :, part], top)
            row_acc[i + x] = best

    def pair(a_ref, i, clcol, prcol, row_acc, b_ref, j, tag_ref, col_acc):
        pairs(a_ref, i, 1, clcol, prcol, row_acc, b_ref, j, 1, tag_ref, col_acc)

    def loop(count, step):
        def each(i, carry):
            step(i)
            return carry

        lax.fori_loop(0, count, each, 0)

    for d in range(stores):
        if d > 0:
            store_copy(d).wait_recv()
            forward(d)
        loop(
            d + 1,
            lambda i, d=d: pair(
                mine, i, clcol_mine, prcol_mine, row_mine, mine, d, tag_mine, col_mine
            ),
        )

    def finish(acc_row, acc_col, d):
        parts = []
        if acc_row is not None:
            parts.append(jnp.max(jnp.transpose(acc_row[d]), axis=0, keepdims=True))
        if acc_col is not None:
            parts.append(jnp.max(acc_col[d], axis=0, keepdims=True))
        return functools.reduce(jnp.maximum, parts)

    def back_copy(kind, src, d):
        where = {"store": in_peer(d)}
        if kind:
            where["blk"] = p + 1 if kind == 1 else p - 1
        return pltpu.make_async_remote_copy(
            src_ref=src.at[d],
            dst_ref=home.at[kind, s],
            send_sem=bk_send.at[kind, d],
            recv_sem=bk_recv.at[kind, s],
            device_id=where,
            device_id_type=MESH,
        )

    @pl.when(use_left)
    def _():
        tag_copy(True).wait_recv()
        for d in range(stores):
            columns(tag_left, clcol_left, prcol_left, d)

    @pl.when(use_right)
    def _():
        tag_copy(False).wait_recv()

    last = stores - 1
    for d in range(last):

        @pl.when(use_right)
        def _(d=d):
            to_left(d).wait_recv()
            loop(
                stores,
                lambda i: pair(
                    mine, i, clcol_mine, prcol_mine, row_mine, right, d, tag_right, col_right
                ),
            )

        @pl.when(use_left)
        def _(d=d):
            to_right(d).wait_recv()
            loop(
                d + 1,
                lambda i: pair(
                    left, i, clcol_left, prcol_left, row_left, right, d, tag_right, col_right
                ),
            )
            if d > 0:
                loop(
                    d,
                    lambda j: pair(
                        left, d, clcol_left, prcol_left, row_left, right, j, tag_right, col_right
                    ),
                )

    @pl.when(use_right)
    def _():
        to_left(last).wait_recv()
        pairs(
            mine, 0, stores, clcol_mine, prcol_mine, row_mine,
            right, last, 1, tag_right, col_right,
        )

    for e in range(stores):
        back_mine[e] = finish(row_mine, col_mine, e)
    for e in range(1, stores):
        back_copy(0, back_mine, e).start()
    home[0, s] = back_mine[0]

    @pl.when(use_left)
    def _():
        to_right(last).wait_recv()
        pairs(
            left, 0, stores, clcol_left, prcol_left, row_left,
            right, last, 1, tag_right, col_right,
        )
        pairs(
            left, last, 1, clcol_left, prcol_left, row_left,
            right, 0, last, tag_right, col_right,
        )

    @pl.when(use_right)
    def _():
        for e in range(stores):
            back_right[e] = finish(None, col_right, e)
            back_copy(1, back_right, e).start()

    @pl.when(use_left)
    def _():
        for e in range(stores):
            back_left[e] = finish(row_left, None, e)
            back_copy(2, back_left, e).start()

    for d in range(1, stores):
        store_copy(d).wait_send()

    @pl.when(give_right)
    def _():
        tag_copy(True).wait_send()
        for d in range(stores):
            to_right(d).wait_send()

    @pl.when(give_left)
    def _():
        tag_copy(False).wait_send()
        for d in range(stores):
            to_left(d).wait_send()

    def arrived(kind, o):
        return pltpu.make_async_remote_copy(
            src_ref=back_mine.at[0],
            dst_ref=home.at[kind, o],
            send_sem=bk_send.at[kind, 0],
            recv_sem=bk_recv.at[kind, o],
            device_id={"store": out_peer(1)},
            device_id_type=MESH,
        )

    for d in range(1, stores):
        back_copy(0, back_mine, d).wait_send()
        arrived(0, out_peer(d)).wait_recv()

    @pl.when(use_right)
    def _():
        for d in range(stores):
            back_copy(1, back_right, d).wait_send()

    @pl.when(use_left)
    def _():
        for d in range(stores):
            back_copy(2, back_left, d).wait_send()

    @pl.when(has_prev)
    def _():
        for o in range(stores):
            arrived(1, o).wait_recv()

    @pl.when(give_right)
    def _():
        for o in range(stores):
            arrived(2, o).wait_recv()

    for o in range(stores):
        out_ref[:, o * send : (o + 1) * send] = jnp.maximum(
            home[0, o], jnp.maximum(home[1, o], home[2, o])
        )


def solution(mesh):
    panels, stores = mesh.shape["blk"], mesh.shape["store"]

    def body(embeddings, slots, clusters, priority):
        rows, width = embeddings.shape
        send = rows // stores
        f32, bf16, i32 = jnp.float32, jnp.bfloat16, jnp.int32
        vm = pltpu.VMEM
        dma = pltpu.SemaphoreType.DMA
        best = pl.pallas_call(
            functools.partial(kernel, panels, stores),
            out_shape=jax.ShapeDtypeStruct((1, rows), f32),
            in_specs=[
                pl.BlockSpec(memory_space=pl.ANY),
                pl.BlockSpec(memory_space=pl.ANY),
                pl.BlockSpec(memory_space=pl.ANY),
                pl.BlockSpec(memory_space=pl.ANY),
            ],
            out_specs=pl.BlockSpec(memory_space=vm),
            scratch_shapes=[
                vm((1, rows), i32),
                vm((1, rows), i32),
                vm((1, rows), i32),
                vm((stores, send, width), f32),
                vm((stores, send, width), bf16),
                vm((stores, send, width), bf16),
                vm((stores, send, width), bf16),
                vm((stores, send, width), bf16),
                vm((stores, 1, send), i32),
                vm((stores, 8, send), f32),
                vm((stores, 8, send), f32),
                vm((stores, 8, send), f32),
                vm((stores, send, 128), f32),
                vm((stores, send, 128), f32),
                vm((stores, send, 128), f32),
                vm((stores, send, 128), f32),
                vm((stores, send, 128), f32),
                vm((stores, send, 128), f32),
                vm((stores, 8, send), f32),
                vm((stores, 8, send), f32),
                vm((stores, 1, send), f32),
                vm((stores, 1, send), f32),
                vm((stores, 1, send), f32),
                vm((3, stores, 1, send), f32),
                dma((stores,)),
                dma((3,)),
                dma((stores,)),
                dma((stores,)),
                dma((stores,)),
                dma((stores,)),
                dma((2,)),
                dma((2,)),
                dma((stores,)),
                dma((stores,)),
                dma((stores,)),
                dma((stores,)),
                dma((3, stores)),
                dma((3, stores)),
            ],
            compiler_params=pltpu.CompilerParams(
                collective_id=0, has_side_effects=True, vmem_limit_bytes=62 * 1024 * 1024
            ),
            name="dedup",
        )(embeddings, slots.reshape(1, rows), clusters, priority)
        return best.reshape(rows)

    return jax.shard_map(
        body,
        mesh=mesh,
        in_specs=(
            P(("groups", "blk", "store"), None),
            P(("groups", "blk", "store")),
            P(("groups", "store"), "blk"),
            P(("groups", "store"), "blk"),
        ),
        out_specs=P(("groups", "blk", "store")),
        check_vma=False,
    )
```

```python
import functools

import jax
import jax.numpy as jnp
from jax import lax
from jax.experimental import pallas as pl
from jax.experimental.pallas import tpu as pltpu
from jax.sharding import PartitionSpec as P

EPS = 1e-06
MESH = pl.DeviceIdType.MESH


def kernel(
    panels,
    stores,
    emb_ref,
    slots_hbm,
    cl_hbm,
    pr_hbm,
    out_ref,
    slots_ref,
    cl_ref,
    pr_ref,
    emb,
    mine,
    left,
    right,
    bound,
    slots_in,
    tag_mine,
    tag_left,
    tag_right,
    clcol_mine,
    prcol_mine,
    clcol_left,
    prcol_left,
    clcol_right,
    prcol_right,
    row_mine,
    row_left,
    row_right,
    col_mine,
    col_left,
    col_right,
    back_mine,
    back_left,
    back_right,
    home,
    load_sem,
    small_sem,
    st_send,
    st_recv,
    sl_send,
    sl_recv,
    tg_send,
    tg_recv,
    zl_send,
    zl_recv,
    zr_send,
    zr_recv,
    bk_send,
    bk_recv,
):
    rows, width = emb.shape
    send = rows // stores
    half = stores // 2
    last = stores - 1
    units = send // 128
    p = lax.axis_index("blk")
    s = lax.axis_index("store")

    def out_peer(d):
        return lax.rem(s // 2 + d // 2, half) * 2 + lax.rem(lax.rem(s, 2) + d % 2, 2)

    def in_peer(d):
        return lax.rem(s // 2 + half - d // 2, half) * 2 + lax.rem(lax.rem(s, 2) + d % 2, 2)

    has_prev = p >= 1
    has_next = p <= panels - 2
    use_right = has_next
    use_left = jnp.logical_and(has_prev, has_next)
    give_right = p <= panels - 3
    give_left = has_prev

    barrier = pltpu.get_barrier_semaphore()
    for d in range(1, stores):
        pl.semaphore_signal(barrier, inc=1, device_id={"store": out_peer(d)}, device_id_type=MESH)

    @pl.when(has_prev)
    def _():
        for d in range(stores):
            pl.semaphore_signal(
                barrier, inc=1, device_id={"blk": p - 1, "store": out_peer(d)}, device_id_type=MESH
            )

    @pl.when(has_next)
    def _():
        for d in range(stores):
            pl.semaphore_signal(
                barrier, inc=1, device_id={"blk": p + 1, "store": out_peer(d)}, device_id_type=MESH
            )

    pieces = [(k * 128, 128) for k in range(units)]
    pieces += [(d * send, send) for d in range(1, last)]
    pieces += [(last * send + k * 128, 128) for k in range(units)]

    def pieces_of(d):
        return [q for q, (first, _) in enumerate(pieces) if first // send == d]

    order = [0, 2, 1] + list(range(3, stores)) if stores > 2 else [0, 1]

    def load(d, k=0):
        count = 128 if d == 0 else send
        source = pl.multiple_of(out_peer(d) * send, send) + k * 128
        return pltpu.make_async_copy(
            emb_ref.at[pl.ds(source, count)],
            emb.at[pl.ds(d * send + k * 128, count)],
            load_sem.at[k if d == 0 else units - 1 + d],
        )

    small = [
        pltpu.make_async_copy(a, b, small_sem.at[k])
        for k, (a, b) in enumerate(
            [(slots_hbm, slots_ref), (cl_hbm, cl_ref), (pr_hbm, pr_ref)]
        )
    ]
    for d in order:
        for k in range(units if d == 0 else 1):
            load(d, k).start()
    for copy in small:
        copy.start()

    low = jnp.full((1, send), -1.0, jnp.float32)
    for k in range(3):
        for o in range(stores):
            home[k, o] = low
    for ref in (row_mine, row_left, row_right):
        ref[...] = jnp.full(ref.shape, -1.0, jnp.float32)
    for ref in (col_mine, col_right, col_left):
        ref[...] = jnp.full(ref.shape, -1.0, jnp.float32)

    def store_copy(d):
        return pltpu.make_async_remote_copy(
            src_ref=bound.at[pl.ds(d * send, send)],
            dst_ref=mine.at[pl.ds(d * send, send)],
            send_sem=st_send.at[d],
            recv_sem=st_recv.at[d],
            device_id={"store": out_peer(d)},
            device_id_type=MESH,
        )

    def slot_copy(d):
        return pltpu.make_async_remote_copy(
            src_ref=slots_ref.at[:, pl.ds(pl.multiple_of(out_peer(d) * send, send), send)],
            dst_ref=slots_in.at[d],
            send_sem=sl_send.at[d],
            recv_sem=sl_recv.at[d],
            device_id={"store": out_peer(d)},
            device_id_type=MESH,
        )

    def to_left(q):
        return pltpu.make_async_remote_copy(
            src_ref=mine.at[pl.ds(*pieces[q])],
            dst_ref=right.at[pl.ds(*pieces[q])],
            send_sem=zl_send.at[q],
            recv_sem=zl_recv.at[q],
            device_id={"blk": p - 1},
            device_id_type=MESH,
        )

    def to_right(q):
        return pltpu.make_async_remote_copy(
            src_ref=mine.at[pl.ds(*pieces[q])],
            dst_ref=left.at[pl.ds(*pieces[q])],
            send_sem=zr_send.at[q],
            recv_sem=zr_recv.at[q],
            device_id={"blk": p + 1},
            device_id_type=MESH,
        )

    def tag_copy(to_next):
        return pltpu.make_async_remote_copy(
            src_ref=tag_mine,
            dst_ref=tag_left if to_next else tag_right,
            send_sem=tg_send.at[1 if to_next else 0],
            recv_sem=tg_recv.at[1 if to_next else 0],
            device_id={"blk": p + 1 if to_next else p - 1},
            device_id_type=MESH,
        )

    def forward(these):
        @pl.when(give_right)
        def _():
            for q in these:
                to_right(q).start()

        @pl.when(give_left)
        def _():
            for q in these:
                to_left(q).start()

    def normalize(first, count, into):
        x = emb[first : first + count, :]
        unit = x * lax.rsqrt(jnp.sum(x * x, axis=1, keepdims=True) + EPS)
        into[first : first + count, :] = unit.astype(jnp.bfloat16)

    for d in order:
        if d == 0:
            for k in range(units):
                load(0, k).wait()
                normalize(k * 128, 128, mine)
                if k == 0:
                    here = jnp.int32(stores - 1)
                    here = here + jnp.where(has_prev, stores, 0) + jnp.where(has_next, stores, 0)
                    pl.semaphore_wait(barrier, here)
                forward([k])
            small[0].wait()
            for e in range(1, stores):
                slot_copy(e).start()
        else:
            load(d).wait()
            normalize(d * send, send, bound)
            store_copy(d).start()

    small[1].wait()
    small[2].wait()
    clusters = cl_ref[...].astype(jnp.float32)
    rank = pr_ref[...]
    upper = (rank // 128).astype(jnp.float32)
    lower = (rank - rank // 128 * 128).astype(jnp.float32)
    line = lax.broadcasted_iota(jnp.int32, (16, rows), 0)
    table = jnp.where(
        line == 0, clusters, jnp.where(line == 1, upper, jnp.where(line == 2, lower, 0.0))
    ).astype(jnp.bfloat16)

    def columns(tag_ref, clcol, prcol, d):
        clcol[d] = jnp.transpose(jnp.broadcast_to(tag_ref[d, 0:1, :], (128, send)))
        prcol[d] = jnp.transpose(jnp.broadcast_to(tag_ref[d, 1:2, :], (128, send)))

    slots_in[0] = slots_ref[:, pl.ds(pl.multiple_of(s * send, send), send)]
    for d in range(stores):
        if d > 0:
            slot_copy(d).wait()
        hot = jnp.where(
            lax.broadcasted_iota(jnp.int32, (rows, send), 0) == slots_in[d], 1.0, 0.0
        ).astype(jnp.bfloat16)
        found = jnp.dot(table, hot, preferred_element_type=jnp.float32)
        tag_mine[d] = jnp.concatenate(
            [found[0:1], found[1:2] * 128.0 + found[2:3], found[2:8]], axis=0
        )
        columns(tag_mine, clcol_mine, prcol_mine, d)

    @pl.when(give_right)
    def _():
        tag_copy(True).start()

    @pl.when(give_left)
    def _():
        tag_copy(False).start()

    def score(a, tags_a, row_acc, b, tags_b, col_acc):
        scores = lax.dot_general(
            a, b, (((1,), (1,)), ((), ())), preferred_element_type=jnp.float32
        )
        cl_r, pr_r = tags_a
        best = row_acc[...]
        for c in range(b.shape[0] // 128):
            cl_q, pr_q = tags_b(c)
            same = jnp.where(cl_r == cl_q, scores[:, c * 128 : (c + 1) * 128], -1.0)
            best = jnp.maximum(best, jnp.where(pr_q < pr_r, same, -1.0))
            other = jnp.where(pr_q > pr_r, same, -1.0)
            col_acc(c, jnp.max(other.reshape(a.shape[0] // 8, 8, 128), axis=0))
        row_acc[...] = best

    def chunk(ref, i):
        return ref[pl.ds(pl.multiple_of(i * send, send), send), :]

    def tags_from(tag_ref, j):
        def at(c):
            part = slice(c % units * 128, c % units * 128 + 128)
            return tag_ref[j + c // units, 0:1, part], tag_ref[j + c // units, 1:2, part]

        return at

    def best_into(acc, j):
        def at(c, top):
            part = slice(c % units * 128, c % units * 128 + 128)
            acc[j + c // units, :, part] = jnp.maximum(acc[j + c // units, :, part], top)

        return at

    def pair(a_ref, i, clcol, prcol, row_acc, b_ref, j, tag_ref, col_acc):
        score(
            chunk(a_ref, i), (clcol[i], prcol[i]), row_acc.at[i],
            chunk(b_ref, j), tags_from(tag_ref, j), best_into(col_acc, j),
        )

    def strip(a_ref, k, clcol, prcol, row_acc, b_ref, count, tag_ref, col_acc):
        part = pl.ds(k * 128, 128)
        score(
            a_ref[last * send + k * 128 : last * send + k * 128 + 128, :],
            (clcol[last, part], prcol[last, part]), row_acc.at[last, part],
            b_ref[0:count, :], tags_from(tag_ref, 0), best_into(col_acc, 0),
        )

    def loop(count, step):
        def each(i, carry):
            step(i)
            return carry

        lax.fori_loop(0, count, each, 0)

    for d in range(stores):
        if d > 0:
            store_copy(d).wait_recv()
            forward(pieces_of(d))
        loop(
            d + 1,
            lambda i, d=d: pair(
                mine, i, clcol_mine, prcol_mine, row_mine, mine, d, tag_mine, col_mine
            ),
        )

    def back_copy(kind, src, d):
        where = {"store": in_peer(d)}
        if kind:
            where["blk"] = p + 1 if kind == 1 else p - 1
        return pltpu.make_async_remote_copy(
            src_ref=src.at[d],
            dst_ref=home.at[kind, s],
            send_sem=bk_send.at[kind, d],
            recv_sem=bk_recv.at[kind, s],
            device_id=where,
            device_id_type=MESH,
        )

    @pl.when(use_left)
    def _():
        tag_copy(True).wait_recv()
        for d in range(stores):
            columns(tag_left, clcol_left, prcol_left, d)

    @pl.when(use_right)
    def _():
        tag_copy(False).wait_recv()
        columns(tag_right, clcol_right, prcol_right, last)

    for d in range(last):

        @pl.when(use_right)
        def _(d=d):
            for q in pieces_of(d):
                to_left(q).wait_recv()
            loop(
                stores,
                lambda i: pair(
                    mine, i, clcol_mine, prcol_mine, row_mine, right, d, tag_right, col_right
                ),
            )

        @pl.when(use_left)
        def _(d=d):
            for q in pieces_of(d):
                to_right(q).wait_recv()
            loop(
                d + 1,
                lambda i: pair(
                    left, i, clcol_left, prcol_left, row_left, right, d, tag_right, col_right
                ),
            )
            if d > 0:
                loop(
                    d,
                    lambda j: pair(
                        left, d, clcol_left, prcol_left, row_left, right, j, tag_right, col_right
                    ),
                )

    def turned(acc, d):
        return jnp.max(jnp.transpose(acc[d]), axis=0, keepdims=True)

    def over_rows(acc, d):
        return jnp.max(acc[d], axis=0, keepdims=True)

    for k, q in enumerate(pieces_of(last)):
        if k == units - 1:
            for e in range(stores):
                back_mine[e] = turned(row_mine, e)
            for e in range(last):
                back_left[e] = turned(row_left, e)

        @pl.when(use_right)
        def _(k=k, q=q):
            to_left(q).wait_recv()
            strip(
                right, k, clcol_right, prcol_right, row_right, mine, rows, tag_mine, col_mine
            )

        @pl.when(use_left)
        def _(k=k, q=q):
            to_right(q).wait_recv()
            strip(
                right, k, clcol_right, prcol_right, row_right,
                left, last * send + k * 128 + 128, tag_left, col_left,
            )
            strip(
                left, k, clcol_left, prcol_left, row_left,
                right, last * send + k * 128, tag_right, col_right,
            )

    for e in range(stores):
        back_mine[e] = jnp.maximum(back_mine[e], over_rows(col_mine, e))
        if e > 0:
            back_copy(0, back_mine, e).start()
    home[0, s] = back_mine[0]

    @pl.when(use_right)
    def _():
        for e in range(stores):
            best = over_rows(col_right, e)
            if e == last:
                best = jnp.maximum(best, turned(row_right, e))
            back_right[e] = best
            back_copy(1, back_right, e).start()

    @pl.when(use_left)
    def _():
        for e in range(stores):
            before = turned(row_left, e) if e == last else back_left[e]
            back_left[e] = jnp.maximum(before, over_rows(col_left, e))
            back_copy(2, back_left, e).start()

    for d in range(1, stores):
        store_copy(d).wait_send()

    @pl.when(give_right)
    def _():
        tag_copy(True).wait_send()
        for q in range(len(pieces)):
            to_right(q).wait_send()

    @pl.when(give_left)
    def _():
        tag_copy(False).wait_send()
        for q in range(len(pieces)):
            to_left(q).wait_send()

    def arrived(kind, o):
        return pltpu.make_async_remote_copy(
            src_ref=back_mine.at[0],
            dst_ref=home.at[kind, o],
            send_sem=bk_send.at[kind, 0],
            recv_sem=bk_recv.at[kind, o],
            device_id={"store": out_peer(1)},
            device_id_type=MESH,
        )

    for d in range(1, stores):
        back_copy(0, back_mine, d).wait_send()
        arrived(0, out_peer(d)).wait_recv()

    @pl.when(use_right)
    def _():
        for d in range(stores):
            back_copy(1, back_right, d).wait_send()

    @pl.when(use_left)
    def _():
        for d in range(stores):
            back_copy(2, back_left, d).wait_send()

    @pl.when(has_prev)
    def _():
        for o in range(stores):
            arrived(1, o).wait_recv()

    @pl.when(give_right)
    def _():
        for o in range(stores):
            arrived(2, o).wait_recv()

    for o in range(stores):
        out_ref[:, o * send : (o + 1) * send] = jnp.maximum(
            home[0, o], jnp.maximum(home[1, o], home[2, o])
        )


def solution(mesh):
    panels, stores = mesh.shape["blk"], mesh.shape["store"]

    def body(embeddings, slots, clusters, priority):
        rows, width = embeddings.shape
        send = rows // stores
        units = send // 128
        f32, bf16, i32 = jnp.float32, jnp.bfloat16, jnp.int32
        vm = pltpu.VMEM
        dma = pltpu.SemaphoreType.DMA
        best = pl.pallas_call(
            functools.partial(kernel, panels, stores),
            out_shape=jax.ShapeDtypeStruct((1, rows), f32),
            in_specs=[
                pl.BlockSpec(memory_space=pl.ANY),
                pl.BlockSpec(memory_space=pl.ANY),
                pl.BlockSpec(memory_space=pl.ANY),
                pl.BlockSpec(memory_space=pl.ANY),
            ],
            out_specs=pl.BlockSpec(memory_space=vm),
            scratch_shapes=[
                vm((1, rows), i32),
                vm((1, rows), i32),
                vm((1, rows), i32),
                vm((rows, width), f32),
                vm((rows, width), bf16),
                vm((rows, width), bf16),
                vm((rows, width), bf16),
                vm((rows, width), bf16),
                vm((stores, 1, send), i32),
                vm((stores, 8, send), f32),
                vm((stores, 8, send), f32),
                vm((stores, 8, send), f32),
                vm((stores, send, 128), f32),
                vm((stores, send, 128), f32),
                vm((stores, send, 128), f32),
                vm((stores, send, 128), f32),
                vm((stores, send, 128), f32),
                vm((stores, send, 128), f32),
                vm((stores, send, 128), f32),
                vm((stores, send, 128), f32),
                vm((stores, send, 128), f32),
                vm((stores, 8, send), f32),
                vm((stores, 8, send), f32),
                vm((stores, 8, send), f32),
                vm((stores, 1, send), f32),
                vm((stores, 1, send), f32),
                vm((stores, 1, send), f32),
                vm((3, stores, 1, send), f32),
                dma((stores + units - 1,)),
                dma((3,)),
                dma((stores,)),
                dma((stores,)),
                dma((stores,)),
                dma((stores,)),
                dma((2,)),
                dma((2,)),
                dma((stores - 2 + 2 * units,)),
                dma((stores - 2 + 2 * units,)),
                dma((stores - 2 + 2 * units,)),
                dma((stores - 2 + 2 * units,)),
                dma((3, stores)),
                dma((3, stores)),
            ],
            compiler_params=pltpu.CompilerParams(
                collective_id=0, has_side_effects=True, vmem_limit_bytes=62 * 1024 * 1024
            ),
            name="dedup",
        )(embeddings, slots.reshape(1, rows), clusters, priority)
        return best.reshape(rows)

    return jax.shard_map(
        body,
        mesh=mesh,
        in_specs=(
            P(("groups", "blk", "store"), None),
            P(("groups", "blk", "store")),
            P(("groups", "store"), "blk"),
            P(("groups", "store"), "blk"),
        ),
        out_specs=P(("groups", "blk", "store")),
        check_vma=False,
    )
```

```python
import functools

import jax
import jax.numpy as jnp
from jax import lax
from jax.experimental import pallas as pl
from jax.experimental.pallas import tpu as pltpu
from jax.sharding import PartitionSpec as P

EPS = 1e-06
MESH = pl.DeviceIdType.MESH


def kernel(
    panels,
    stores,
    emb_ref,
    slots_hbm,
    cl_hbm,
    pr_hbm,
    out_ref,
    slots_ref,
    cl_ref,
    pr_ref,
    emb,
    mine,
    left,
    right,
    bound,
    slots_in,
    tag_mine,
    tag_left,
    tag_right,
    clcol_mine,
    prcol_mine,
    clcol_left,
    prcol_left,
    clcol_right,
    prcol_right,
    row_mine,
    row_left,
    row_right,
    col_mine,
    col_left,
    col_right,
    back_mine,
    back_left,
    back_right,
    home,
    load_sem,
    small_sem,
    st_send,
    st_recv,
    sl_send,
    sl_recv,
    tg_send,
    tg_recv,
    zl_send,
    zl_recv,
    zr_send,
    zr_recv,
    bk_send,
    bk_recv,
):
    rows, width = emb.shape
    send = rows // stores
    half = stores // 2
    last = stores - 1
    units = send // 128
    p = lax.axis_index("blk")
    s = lax.axis_index("store")

    def out_peer(d):
        return lax.rem(s // 2 + d // 2, half) * 2 + lax.rem(lax.rem(s, 2) + d % 2, 2)

    def in_peer(d):
        return lax.rem(s // 2 + half - d // 2, half) * 2 + lax.rem(lax.rem(s, 2) + d % 2, 2)

    has_prev = p >= 1
    has_next = p <= panels - 2
    use_right = has_next
    use_left = has_prev
    use_both = jnp.logical_and(has_prev, has_next)
    give_right = has_next
    give_left = has_prev

    barrier = pltpu.get_barrier_semaphore()
    for d in range(1, stores):
        pl.semaphore_signal(barrier, inc=1, device_id={"store": out_peer(d)}, device_id_type=MESH)

    @pl.when(has_prev)
    def _():
        for d in range(stores):
            pl.semaphore_signal(
                barrier, inc=1, device_id={"blk": p - 1, "store": out_peer(d)}, device_id_type=MESH
            )

    @pl.when(has_next)
    def _():
        for d in range(stores):
            pl.semaphore_signal(
                barrier, inc=1, device_id={"blk": p + 1, "store": out_peer(d)}, device_id_type=MESH
            )

    pieces = [(k * 128, 128) for k in range(units)]
    pieces += [(d * send, send) for d in range(1, last)]
    pieces += [(last * send + k * 128, 128) for k in range(units)]

    def pieces_of(d):
        return [q for q, (first, _) in enumerate(pieces) if first // send == d]

    order = [0, 2, 1] + list(range(3, stores)) if stores > 2 else [0, 1]

    def load(d, k=0):
        count = 128 if d == 0 else send
        source = pl.multiple_of(out_peer(d) * send, send) + k * 128
        return pltpu.make_async_copy(
            emb_ref.at[pl.ds(source, count)],
            emb.at[pl.ds(d * send + k * 128, count)],
            load_sem.at[k if d == 0 else units - 1 + d],
        )

    small = [
        pltpu.make_async_copy(a, b, small_sem.at[k])
        for k, (a, b) in enumerate(
            [(slots_hbm, slots_ref), (cl_hbm, cl_ref), (pr_hbm, pr_ref)]
        )
    ]
    for d in order:
        for k in range(units if d == 0 else 1):
            load(d, k).start()
    for copy in small:
        copy.start()

    low = jnp.full((1, send), -1.0, jnp.float32)
    for k in range(3):
        for o in range(stores):
            home[k, o] = low
    for ref in (row_mine, row_left, row_right):
        ref[...] = jnp.full(ref.shape, -1.0, jnp.float32)
    for ref in (col_mine, col_right, col_left):
        ref[...] = jnp.full(ref.shape, -1.0, jnp.float32)

    def store_copy(d):
        return pltpu.make_async_remote_copy(
            src_ref=bound.at[pl.ds(d * send, send)],
            dst_ref=mine.at[pl.ds(d * send, send)],
            send_sem=st_send.at[d],
            recv_sem=st_recv.at[d],
            device_id={"store": out_peer(d)},
            device_id_type=MESH,
        )

    def slot_copy(d):
        return pltpu.make_async_remote_copy(
            src_ref=slots_ref.at[:, pl.ds(pl.multiple_of(out_peer(d) * send, send), send)],
            dst_ref=slots_in.at[d],
            send_sem=sl_send.at[d],
            recv_sem=sl_recv.at[d],
            device_id={"store": out_peer(d)},
            device_id_type=MESH,
        )

    def to_left(q):
        return pltpu.make_async_remote_copy(
            src_ref=mine.at[pl.ds(*pieces[q])],
            dst_ref=right.at[pl.ds(*pieces[q])],
            send_sem=zl_send.at[q],
            recv_sem=zl_recv.at[q],
            device_id={"blk": p - 1},
            device_id_type=MESH,
        )

    def to_right(q):
        return pltpu.make_async_remote_copy(
            src_ref=mine.at[pl.ds(*pieces[q])],
            dst_ref=left.at[pl.ds(*pieces[q])],
            send_sem=zr_send.at[q],
            recv_sem=zr_recv.at[q],
            device_id={"blk": p + 1},
            device_id_type=MESH,
        )

    def tag_copy(to_next):
        return pltpu.make_async_remote_copy(
            src_ref=tag_mine,
            dst_ref=tag_left if to_next else tag_right,
            send_sem=tg_send.at[1 if to_next else 0],
            recv_sem=tg_recv.at[1 if to_next else 0],
            device_id={"blk": p + 1 if to_next else p - 1},
            device_id_type=MESH,
        )

    waited = set()

    def forward(these, after=()):
        waited.update(after)

        @pl.when(give_right)
        def _():
            for q in after:
                to_right(q).wait_send()
            for q in these:
                to_right(q).start()

        @pl.when(give_left)
        def _():
            for q in after:
                to_left(q).wait_send()
            for q in these:
                to_left(q).start()

    def normalize(first, count, into):
        x = emb[first : first + count, :]
        unit = x * lax.rsqrt(jnp.sum(x * x, axis=1, keepdims=True) + EPS)
        into[first : first + count, :] = unit.astype(jnp.bfloat16)

    for d in order:
        if d == 0:
            for k in range(units):
                load(0, k).wait()
                normalize(k * 128, 128, mine)
                if k == 0:
                    here = jnp.int32(stores - 1)
                    here = here + jnp.where(has_prev, stores, 0) + jnp.where(has_next, stores, 0)
                    pl.semaphore_wait(barrier, here)
                forward([k])
            small[0].wait()
            for e in range(1, stores):
                slot_copy(e).start()
        else:
            load(d).wait()
            normalize(d * send, send, bound)
            if d <= 2:
                store_copy(d).start()

    small[1].wait()
    small[2].wait()
    clusters = cl_ref[...].astype(jnp.float32)
    rank = pr_ref[...]
    upper = (rank // 128).astype(jnp.float32)
    lower = (rank - rank // 128 * 128).astype(jnp.float32)
    line = lax.broadcasted_iota(jnp.int32, (16, rows), 0)
    table = jnp.where(
        line == 0, clusters, jnp.where(line == 1, upper, jnp.where(line == 2, lower, 0.0))
    ).astype(jnp.bfloat16)

    def columns(tag_ref, clcol, prcol, d):
        clcol[d] = jnp.transpose(jnp.broadcast_to(tag_ref[d, 0:1, :], (128, send)))
        prcol[d] = jnp.transpose(jnp.broadcast_to(tag_ref[d, 1:2, :], (128, send)))

    slots_in[0] = slots_ref[:, pl.ds(pl.multiple_of(s * send, send), send)]
    for d in range(stores):
        if d > 0:
            slot_copy(d).wait()
        hot = jnp.where(
            lax.broadcasted_iota(jnp.int32, (rows, send), 0) == slots_in[d], 1.0, 0.0
        ).astype(jnp.bfloat16)
        found = jnp.dot(table, hot, preferred_element_type=jnp.float32)
        tag_mine[d] = jnp.concatenate(
            [found[0:1], found[1:2] * 128.0 + found[2:3], found[2:8]], axis=0
        )
        columns(tag_mine, clcol_mine, prcol_mine, d)

    @pl.when(give_right)
    def _():
        tag_copy(True).start()

    @pl.when(give_left)
    def _():
        tag_copy(False).start()

    def score(a, tags_a, row_acc, b, tags_b, col_acc):
        scores = lax.dot_general(
            a, b, (((1,), (1,)), ((), ())), preferred_element_type=jnp.float32
        )
        cl_r, pr_r = tags_a
        best = row_acc[...]
        for c in range(b.shape[0] // 128):
            cl_q, pr_q = tags_b(c)
            same = jnp.where(cl_r == cl_q, scores[:, c * 128 : (c + 1) * 128], -1.0)
            best = jnp.maximum(best, jnp.where(pr_q < pr_r, same, -1.0))
            other = jnp.where(pr_q > pr_r, same, -1.0)
            col_acc(c, jnp.max(other.reshape(a.shape[0] // 8, 8, 128), axis=0))
        row_acc[...] = best

    def chunk(ref, i):
        return ref[pl.ds(pl.multiple_of(i * send, send), send), :]

    def tags_from(tag_ref, j):
        def at(c):
            part = slice(c % units * 128, c % units * 128 + 128)
            return tag_ref[j + c // units, 0:1, part], tag_ref[j + c // units, 1:2, part]

        return at

    def best_into(acc, j):
        def at(c, top):
            part = slice(c % units * 128, c % units * 128 + 128)
            acc[j + c // units, :, part] = jnp.maximum(acc[j + c // units, :, part], top)

        return at

    def pair(a_ref, i, clcol, prcol, row_acc, b_ref, j, tag_ref, col_acc):
        score(
            chunk(a_ref, i), (clcol[i], prcol[i]), row_acc.at[i],
            chunk(b_ref, j), tags_from(tag_ref, j), best_into(col_acc, j),
        )

    def strip(a_ref, k, clcol, prcol, row_acc, b_ref, j, first, count, tag_ref, col_acc):
        part = pl.ds(k * 128, 128)
        score(
            a_ref[last * send + k * 128 : last * send + k * 128 + 128, :],
            (clcol[last, part], prcol[last, part]), row_acc.at[last, part],
            b_ref[first : first + count, :], tags_from(tag_ref, j), best_into(col_acc, j),
        )

    def loop(count, step):
        def each(i, carry):
            step(i)
            return carry

        lax.fori_loop(0, count, each, 0)

    for d in range(stores):
        if d > 0:
            if 2 <= d < last:
                store_copy(d).wait_send()
                store_copy(d + 1).start()
            store_copy(d).wait_recv()
            if d < last:
                forward(pieces_of(d))
        loop(
            d + 1,
            lambda i, d=d: pair(
                mine, i, clcol_mine, prcol_mine, row_mine, mine, d, tag_mine, col_mine
            ),
        )

    def back_copy(kind, src, d):
        where = {"store": in_peer(d)}
        if kind:
            where["blk"] = p + 1 if kind == 1 else p - 1
        return pltpu.make_async_remote_copy(
            src_ref=src.at[d],
            dst_ref=home.at[kind, s],
            send_sem=bk_send.at[kind, d],
            recv_sem=bk_recv.at[kind, s],
            device_id=where,
            device_id_type=MESH,
        )

    @pl.when(use_left)
    def _():
        tag_copy(True).wait_recv()
        for d in range(stores):
            columns(tag_left, clcol_left, prcol_left, d)

    @pl.when(use_right)
    def _():
        tag_copy(False).wait_recv()
        columns(tag_right, clcol_right, prcol_right, last)

    for d in range(last):
        if d == last - 2:
            forward(pieces_of(last)[:1], pieces_of(d))
        if d == last - 1:
            forward(pieces_of(last)[1:], pieces_of(d))

        @pl.when(use_right)
        def _(d=d):
            for q in pieces_of(d):
                to_left(q).wait_recv()
            loop(
                stores,
                lambda i: pair(
                    mine, i, clcol_mine, prcol_mine, row_mine, right, d, tag_right, col_right
                ),
            )

        @pl.when(use_left)
        def _(d=d):
            for q in pieces_of(d):
                to_right(q).wait_recv()
            pair(left, d, clcol_left, prcol_left, row_left, mine, last, tag_mine, col_mine)

        @pl.when(use_both)
        def _(d=d):
            loop(
                d + 1,
                lambda i: pair(
                    left, i, clcol_left, prcol_left, row_left, right, d, tag_right, col_right
                ),
            )
            if d > 0:
                loop(
                    d,
                    lambda j: pair(
                        left, d, clcol_left, prcol_left, row_left, right, j, tag_right, col_right
                    ),
                )

    def turned(acc, d):
        return jnp.max(jnp.transpose(acc[d]), axis=0, keepdims=True)

    def over_rows(acc, d):
        return jnp.max(acc[d], axis=0, keepdims=True)

    for k, q in enumerate(pieces_of(last)):
        if k == units - 1:
            for e in range(stores):
                back_mine[e] = turned(row_mine, e)
            for e in range(last):
                back_left[e] = turned(row_left, e)

        @pl.when(use_right)
        def _(q=q):
            to_left(q).wait_recv()

        @pl.when(use_left)
        def _(k=k, q=q):
            to_right(q).wait_recv()
            strip(
                left, k, clcol_left, prcol_left, row_left,
                mine, last, last * send, send, tag_mine, col_mine,
            )

        @pl.when(use_both)
        def _(k=k):
            strip(
                right, k, clcol_right, prcol_right, row_right,
                left, 0, 0, last * send + k * 128 + 128, tag_left, col_left,
            )
            strip(
                left, k, clcol_left, prcol_left, row_left,
                right, 0, 0, last * send + k * 128, tag_right, col_right,
            )

    for e in range(stores):
        back_mine[e] = jnp.maximum(back_mine[e], over_rows(col_mine, e))
        if e > 0:
            back_copy(0, back_mine, e).start()
    home[0, s] = back_mine[0]

    @pl.when(use_right)
    def _():
        for e in range(stores):
            best = over_rows(col_right, e)
            if e == last:
                best = jnp.maximum(best, turned(row_right, e))
            back_right[e] = best
            back_copy(1, back_right, e).start()

    @pl.when(use_left)
    def _():
        for e in range(stores):
            before = turned(row_left, e) if e == last else back_left[e]
            back_left[e] = jnp.maximum(before, over_rows(col_left, e))
            back_copy(2, back_left, e).start()

    for d in range(1, stores):
        if d < 2 or d == last:
            store_copy(d).wait_send()

    @pl.when(give_right)
    def _():
        tag_copy(True).wait_send()
        for q in range(len(pieces)):
            if q not in waited:
                to_right(q).wait_send()

    @pl.when(give_left)
    def _():
        tag_copy(False).wait_send()
        for q in range(len(pieces)):
            if q not in waited:
                to_left(q).wait_send()

    def arrived(kind, o):
        return pltpu.make_async_remote_copy(
            src_ref=back_mine.at[0],
            dst_ref=home.at[kind, o],
            send_sem=bk_send.at[kind, 0],
            recv_sem=bk_recv.at[kind, o],
            device_id={"store": out_peer(1)},
            device_id_type=MESH,
        )

    for d in range(1, stores):
        back_copy(0, back_mine, d).wait_send()
        arrived(0, out_peer(d)).wait_recv()

    @pl.when(use_right)
    def _():
        for d in range(stores):
            back_copy(1, back_right, d).wait_send()

    @pl.when(use_left)
    def _():
        for d in range(stores):
            back_copy(2, back_left, d).wait_send()

    @pl.when(has_prev)
    def _():
        for o in range(stores):
            arrived(1, o).wait_recv()

    @pl.when(give_right)
    def _():
        for o in range(stores):
            arrived(2, o).wait_recv()

    for o in range(stores):
        out_ref[:, o * send : (o + 1) * send] = jnp.maximum(
            home[0, o], jnp.maximum(home[1, o], home[2, o])
        )


def solution(mesh):
    panels, stores = mesh.shape["blk"], mesh.shape["store"]

    def body(embeddings, slots, clusters, priority):
        rows, width = embeddings.shape
        send = rows // stores
        units = send // 128
        f32, bf16, i32 = jnp.float32, jnp.bfloat16, jnp.int32
        vm = pltpu.VMEM
        dma = pltpu.SemaphoreType.DMA
        best = pl.pallas_call(
            functools.partial(kernel, panels, stores),
            out_shape=jax.ShapeDtypeStruct((1, rows), f32),
            in_specs=[
                pl.BlockSpec(memory_space=pl.ANY),
                pl.BlockSpec(memory_space=pl.ANY),
                pl.BlockSpec(memory_space=pl.ANY),
                pl.BlockSpec(memory_space=pl.ANY),
            ],
            out_specs=pl.BlockSpec(memory_space=vm),
            scratch_shapes=[
                vm((1, rows), i32),
                vm((1, rows), i32),
                vm((1, rows), i32),
                vm((rows, width), f32),
                vm((rows, width), bf16),
                vm((rows, width), bf16),
                vm((rows, width), bf16),
                vm((rows, width), bf16),
                vm((stores, 1, send), i32),
                vm((stores, 8, send), f32),
                vm((stores, 8, send), f32),
                vm((stores, 8, send), f32),
                vm((stores, send, 128), f32),
                vm((stores, send, 128), f32),
                vm((stores, send, 128), f32),
                vm((stores, send, 128), f32),
                vm((stores, send, 128), f32),
                vm((stores, send, 128), f32),
                vm((stores, send, 128), f32),
                vm((stores, send, 128), f32),
                vm((stores, send, 128), f32),
                vm((stores, 8, send), f32),
                vm((stores, 8, send), f32),
                vm((stores, 8, send), f32),
                vm((stores, 1, send), f32),
                vm((stores, 1, send), f32),
                vm((stores, 1, send), f32),
                vm((3, stores, 1, send), f32),
                dma((stores + units - 1,)),
                dma((3,)),
                dma((stores,)),
                dma((stores,)),
                dma((stores,)),
                dma((stores,)),
                dma((2,)),
                dma((2,)),
                dma((stores - 2 + 2 * units,)),
                dma((stores - 2 + 2 * units,)),
                dma((stores - 2 + 2 * units,)),
                dma((stores - 2 + 2 * units,)),
                dma((3, stores)),
                dma((3, stores)),
            ],
            compiler_params=pltpu.CompilerParams(
                collective_id=0, has_side_effects=True, vmem_limit_bytes=62 * 1024 * 1024
            ),
            name="dedup",
        )(embeddings, slots.reshape(1, rows), clusters, priority)
        return best.reshape(rows)

    return jax.shard_map(
        body,
        mesh=mesh,
        in_specs=(
            P(("groups", "blk", "store"), None),
            P(("groups", "blk", "store")),
            P(("groups", "store"), "blk"),
            P(("groups", "store"), "blk"),
        ),
        out_specs=P(("groups", "blk", "store")),
        check_vma=False,
    )
```
